32 devices in a mesh: bi: 4 (over y, x), bj: 4 (over z), sl: 2 (over core).
Axes of the slice: x: 2, y: 2, z: 4, core: 2. Of those that a mesh axis runs over, the one named last changes fastest.
Arguments:
- snapshots: bfloat16 [2048, 3072], P('sl', ('bj', 'bi')), may hold values from -6 to 6
- slot_map: int32 [16, 192], P(('bj', 'bi')), may hold values from 0 to 191, each once within a row
- row_weight: float32 [2048], P('sl'), may hold values from 0.00048828125 to 0.0078125
- valid_rows: int32 [2, 4], P('sl'), may hold values from 1 to 256, 768 in all within a row
Outputs:
- gram: float32 [3072, 3072], P(('bi', 'sl'), 'bj')
The draws below stay inside these ranges and needn't reach their ends.
Inputs may be any that keep to these rules, and one draw needn't show every extreme that they name: Each row of slot_map is a permutation of 0 to 191. Each row of valid_rows sums to 768, and holds one count equal to 256.
All inputs are finite; a program needn't handle non-finite values.
Results may differ from the reference program's by a relative error of at most 0.0028.
Values may be sent and summed in bfloat16 or wider, within the bound.
A program may use at most 128 MiB of HBM per device.

```python
import math
import jax
import jax.numpy as jnp
import numpy as np
from jax import lax

SHARD = 192
SOURCES = 4
SRC_ROWS = 256
ROWS_DEV = 1024
ROWS = 2048
NSNAP = 3072
N_SL = 2


def levels(key, shape, pieces, smallest, largest):
    def one(position, parts):
        heights = jax.random.uniform(jax.random.fold_in(jax.random.fold_in(key, 6), position), (parts,), jnp.float32, smallest / len(pieces), largest / len(pieces))
        return jnp.repeat(jnp.exp(heights), shape[position] // parts).reshape((-1,) + (1,) * (len(shape) - position - 1))

    factor_of = one(*pieces[0])
    for cut in pieces[1:]:
        factor_of = factor_of * one(*cut)
    return factor_of


def split_up(count, total, most, slope):
    portions = [(1 << 20) // math.isqrt(grade ** slope) + 1 for grade in range(2, count + 1)]
    rest, holding = total - most - (count - 1), [1] * (count - 1)
    while rest > 0:
        free = [i for i in range(count - 1) if holding[i] < most]
        pool, budget = sum([portions[i] for i in free]), rest
        for i in free:
            extra = min(most - holding[i], max(1, budget * portions[i] // pool), rest)
            holding[i] = holding[i] + extra
            rest = rest - extra
    return np.array([most] + holding)


def uneven_parts(rng, amount, total, reach, skew):
    if amount == 2:
        one = jax.random.randint(rng, (), max(1, total - reach), min(reach, total - 1) + 1)
        return jnp.stack([one, total - one])
    lengths = jnp.asarray(split_up(amount, total, reach, skew), jnp.int32)
    pairs = (amount - 1) // 2
    source_of, taker = lengths[1:1 + 2 * pairs:2], lengths[2:2 + 2 * pairs:2]
    slack = jnp.minimum(source_of - 1, reach - taker)
    passed = jax.random.randint(jax.random.fold_in(rng, 1), (pairs,), 0, 1 << 20) % (slack + 1)
    lengths = lengths.at[1:1 + 2 * pairs:2].set(source_of - passed).at[2:2 + 2 * pairs:2].set(taker + passed)
    return lengths[jax.random.permutation(jax.random.fold_in(rng, 2), amount)]


def bell_draw(rng, extent, deviation, reach, split=(), held_as=jnp.bfloat16):
    entries = deviation * jax.random.normal(rng, extent, jnp.float32)
    if split:
        entries = entries * levels(rng, extent, split, -0.22, 0.18)
    return jnp.clip(entries, -reach, reach).astype(held_as)


def setup_inputs(seed: int = 0) -> dict:
    seeds = jax.random.split(jax.random.key(seed), 5)
    snapshots = bell_draw(seeds[0], (ROWS, NSNAP), 1.0, 6.0, ((0, 2), (1, 16)))
    slot_map = jax.vmap(lambda own: jax.random.permutation(own, SHARD))(jax.random.split(seeds[1], (NSNAP // SHARD))).reshape((NSNAP // SHARD, SHARD)).astype(jnp.int32)
    row_weight = jnp.clip(jnp.exp(math.log(0.0078125) - 2.7725887 * jax.random.uniform(seeds[2], (ROWS,), jnp.float32) ** levels(seeds[2], (ROWS,), ((0, 2),), -0.2, 0.2)), 0.00048828125, 0.0078125)
    valid_rows = jax.vmap(lambda own: uneven_parts(own, SOURCES, 3 * SRC_ROWS, SRC_ROWS, 1))(jax.random.split(seeds[3], N_SL)).reshape((N_SL, SOURCES)).astype(jnp.int32)
    return {"snapshots": snapshots, "slot_map": slot_map, "row_weight": row_weight, "valid_rows": valid_rows}


def reference(snapshots, slot_map, row_weight, valid_rows):
    blocks = slot_map.shape[0]
    target = (jnp.arange(blocks, dtype=jnp.int32)[:, None] * SHARD + slot_map).reshape(-1).astype(jnp.int32)
    ordered = jnp.zeros_like(snapshots).at[:, target].set(snapshots)
    positions = jnp.arange(ROWS, dtype=jnp.int32)
    slab_half = positions // ROWS_DEV
    source = (positions % ROWS_DEV) // SRC_ROWS
    within = positions % SRC_ROWS
    row_limit = valid_rows[slab_half, source]
    row_factor = jnp.where(within < row_limit, row_weight, jnp.zeros_like(row_weight))
    weighted = (ordered.astype(jnp.float32) * row_factor[:, None]).astype(jnp.bfloat16)
    return lax.dot_general(weighted, ordered, (((0,), (0,)), ((), ())), preferred_element_type=jnp.float32)
```

```python
import jax
import jax.numpy as jnp
from jax import lax
from jax.experimental import pallas as pl
from jax.experimental.pallas import tpu as pltpu
from jax.sharding import PartitionSpec as P

MESH = pl.DeviceIdType.MESH
CHUNKS = 4


def nt(a, b):
    return lax.dot_general(a, b, (((1,), (1,)), ((), ())), preferred_element_type=jnp.float32)


def contract_rows(left_panel, right_panel):
    return lax.dot_general(
        left_panel, right_panel, (((0,), (0,)), ((), ())), preferred_element_type=jnp.float32
    )


def body(snapshots, slot_map, row_weight, valid_rows):
    local_rows = snapshots.shape[0]
    sources_here = valid_rows.shape[1]
    source_rows = local_rows // sources_here
    ordered = jnp.zeros_like(snapshots).at[:, slot_map[0]].set(snapshots)
    positions = jnp.arange(local_rows, dtype=jnp.int32)
    source = positions // source_rows
    within = positions % source_rows
    source_ids = jnp.arange(sources_here, dtype=jnp.int32)
    matches = source[:, None] == source_ids[None, :]
    row_limit = jnp.sum(jnp.where(matches, valid_rows[0][None, :], 0), axis=1)
    row_factor = jnp.where(within < row_limit, row_weight, jnp.zeros_like(row_weight))
    count_bi = lax.axis_size("bi")
    count_bj = lax.axis_size("bj")
    per_row = count_bj // count_bi
    row_count = ordered.shape[0]
    shard_width = ordered.shape[1]
    column_panel = lax.all_gather(ordered, "bi", axis=1, tiled=True)
    weighted_shard = (ordered.astype(jnp.float32) * row_factor[:, None]).astype(jnp.bfloat16)
    sectioned = weighted_shard.reshape(row_count, 1, 1, shard_width)
    moved = lax.all_to_all(
        lax.all_to_all(sectioned, "bj", split_axis=0, concat_axis=1, tiled=True),
        "bi",
        split_axis=1,
        concat_axis=2,
        tiled=True,
    )
    gathered = lax.all_gather(moved, "bj", axis=0, tiled=True)
    weighted = gathered.reshape(row_count, per_row * count_bi * shard_width)
    return lax.psum_scatter(
        contract_rows(weighted, column_panel), "sl", scatter_dimension=0, tiled=True
    )


def gram_kernel(
    snap, slot, weight, valid, out,
    colp, rowp, offl, wrow, acc, other,
    own_z, gsend, grecv, upsend, dnsend, rrecv, orecv, psend, ssend, srecv,
):
    r = lax.axis_index("bi")
    z = lax.axis_index("bj")
    s = lax.axis_index("sl")
    rows, width = snap.shape
    sources = valid.shape[1]
    src_rows = rows // sources
    kept = (sources - 1) * src_rows
    C = CHUNKS
    part = width // C
    diag = r == z
    not_diag = r != z
    low = z > 0
    high = z < 3

    barrier = pltpu.get_barrier_semaphore()
    for k in (1, 2, 3):
        mate = (r + k) % 4
        pl.semaphore_signal(barrier, inc=1, device_id={"bi": mate}, device_id_type=MESH)
    pl.semaphore_signal(barrier, inc=1, device_id={"sl": 1 - s}, device_id_type=MESH)

    @pl.when(low)
    def _():
        pl.semaphore_signal(barrier, inc=1, device_id={"bj": z - 1}, device_id_type=MESH)

    @pl.when(high)
    def _():
        pl.semaphore_signal(barrier, inc=1, device_id={"bj": z + 1}, device_id_type=MESH)

    place = lax.broadcasted_iota(jnp.int32, (width, width), 0)
    turn = (place == slot[...]).astype(jnp.float32).astype(jnp.bfloat16)
    turned = nt(turn, snap[...]).astype(jnp.bfloat16)
    start = jnp.int32(0)
    targets = []
    lane = lax.broadcasted_iota(jnp.int32, (1, src_rows), 1)
    for q in range(sources):
        count = valid[0, q]
        targets.append(jnp.where(lane < count, lane + start, -1))
        start = start + count
    target = jnp.concatenate(targets, axis=1)
    choose = (lax.broadcasted_iota(jnp.int32, (kept, rows), 0) == target)
    choose = choose.astype(jnp.float32).astype(jnp.bfloat16)
    w = weight[...].reshape(1, rows)
    hi = w.astype(jnp.bfloat16).astype(jnp.float32)
    mid = (w - hi).astype(jnp.bfloat16).astype(jnp.float32)
    low_bits = w - hi - mid
    pieces = jnp.concatenate([hi, mid, low_bits, jnp.zeros((13, rows), jnp.float32)], axis=0)
    packed = nt(jnp.concatenate([turned, pieces.astype(jnp.bfloat16)], axis=0), choose)
    colp[pl.ds(r, 1)] = packed[:width].astype(jnp.bfloat16).reshape(1, C, part, kept)
    wrow[...] = packed[width:width + 1] + packed[width + 1:width + 2] + packed[width + 2:width + 3]

    pl.semaphore_wait(barrier, 4 + (z + 3) // 4 + (6 - z) // 4)

    def to_plane(k, c):
        return pltpu.make_async_remote_copy(
            src_ref=colp.at[r, c], dst_ref=colp.at[r, c],
            send_sem=gsend.at[k, c], recv_sem=grecv.at[r, c],
            device_id={"bi": flip(k)}, device_id_type=MESH)

    def flip(k):
        x, y = r % 2, r // 2
        x = 1 - x if k % 2 else x
        y = 1 - y if k // 2 else y
        return 2 * y + x

    def along(src, dst, step, sends, recvs, b, c):
        return pltpu.make_async_remote_copy(
            src_ref=src.at[b, c], dst_ref=dst.at[b, c],
            send_sem=sends.at[b, c], recv_sem=recvs.at[b, c],
            device_id={"bj": z + step}, device_id_type=MESH)

    def up_row(src, b, c):
        return along(src, rowp, 1, upsend, rrecv, b, c)

    def dn_row(src, b, c):
        return along(src, rowp, -1, dnsend, rrecv, b, c)

    def own_off(step, sends, c):
        return pltpu.make_async_remote_copy(
            src_ref=colp.at[r, c], dst_ref=offl.at[z, c],
            send_sem=sends.at[z, c], recv_sem=orecv.at[z, c],
            device_id={"bj": z + step}, device_id_type=MESH)

    def hand(p, c):
        return pltpu.make_async_remote_copy(
            src_ref=offl.at[p, c], dst_ref=rowp.at[r, c],
            send_sem=psend.at[p, c], recv_sem=rrecv.at[r, c],
            device_id={"bi": p}, device_id_type=MESH)

    def got(buf, recvs, b, c):
        pltpu.make_async_remote_copy(
            src_ref=buf.at[b, c], dst_ref=buf.at[b, c],
            send_sem=own_z.at[0], recv_sem=recvs.at[b, c],
            device_id={"sl": 1 - s}, device_id_type=MESH).wait_recv()

    def act(condition, copy, drain):
        @pl.when(condition)
        def _():
            if drain:
                copy().wait_send()
            else:
                copy().start()

    down = (r - z + 3 + r // 3) // 4
    second = down * (3 - r // 3) + (1 - down) * (1 - (r + 2) // 3)
    third = down * 6 + (1 - down) * 3 - r - second
    lent = (1 - down) * 3
    natural = (r, second, third)
    off_down = (r == 0)
    off_up = (r == 3)

    def send_own(c, drain):
        act(diag & low, lambda: dn_row(colp, r, c), drain)
        act(diag & high, lambda: up_row(colp, r, c), drain)
        act(off_down & low, lambda: own_off(-1, dnsend, c), drain)
        act(off_up & high, lambda: own_off(1, upsend, c), drain)
        for k in (1, 2):
            act(r >= 0, lambda: to_plane(k, c), drain)

    def send_far(c, drain):
        act(r >= 0, lambda: to_plane(3, c), drain)

    def plane_step(k, c, drain):
        b = flip(k)
        if not drain:
            got(colp, grecv, b, c)
        act(diag & low & (b >= 1), lambda: dn_row(colp, b, c), drain)
        act(diag & high & (b <= 2), lambda: up_row(colp, b, c), drain)

    def line_step(u, c, drain):
        b = natural[u]

        @pl.when(not_diag)
        def _():
            if not drain:
                got(rowp, rrecv, b, c)
        act((z < r) & low, lambda: dn_row(rowp, b, c), drain)
        act((z > r) & high, lambda: up_row(rowp, b, c), drain)

        p_dn = z + 1 + u

        @pl.when(off_down & (p_dn <= 3))
        def _():
            if not drain:
                got(offl, orecv, p_dn, c)
            act(low, lambda: along(offl, offl, -1, dnsend, orecv, p_dn, c), drain)
            act(r >= 0, lambda: hand(p_dn, c), drain)

        p_up = z - 1 - u

        @pl.when(off_up & (p_up >= 0))
        def _():
            if not drain:
                got(offl, orecv, p_up, c)
            act(high, lambda: along(offl, offl, 1, upsend, orecv, p_up, c), drain)
            act(r >= 0, lambda: hand(p_up, c), drain)

    def over(step):
        def one(c, carry):
            step(c)
            return carry
        lax.fori_loop(0, C, one, 0)

    def to_sister(b):
        return pltpu.make_async_remote_copy(
            src_ref=acc.at[b], dst_ref=other.at[b % 2],
            send_sem=ssend.at[b % 2], recv_sem=srecv.at[b % 2],
            device_id={"sl": 1 - s}, device_id_type=MESH)

    def multiply(b):
        @pl.when(diag)
        def _():
            rowp[pl.ds(b, 1)] = colp[pl.ds(b, 1)]
        block = rowp[pl.ds(b, 1)].reshape(width, kept).astype(jnp.float32)
        weighted = (block * wrow[...]).astype(jnp.bfloat16)
        acc[pl.ds(b, 1)] = nt(weighted, colp[...].reshape(4 * width, kept))[None]

        @pl.when(b // 2 != s)
        def _():
            to_sister(b).start()

    over(lambda c: send_own(c, False))
    over(lambda c: send_far(c, False))

    def first(c):
        plane_step(1, c, False)
        plane_step(2, c, False)
        line_step(0, c, False)
    over(first)

    def middle(c):
        plane_step(3, c, False)
        line_step(1, c, False)
    over(middle)
    multiply(natural[0])
    multiply(natural[1])
    over(lambda c: line_step(2, c, False))
    multiply(natural[2])

    def last(c):
        @pl.when(not_diag)
        def _():
            got(rowp, rrecv, lent, c)
    over(last)
    multiply(lent)

    for j in range(2):
        pltpu.make_async_remote_copy(
            src_ref=acc.at[j], dst_ref=other.at[j], send_sem=ssend.at[j], recv_sem=srecv.at[j],
            device_id={"sl": 1 - s}, device_id_type=MESH).wait()
        out[j * width:(j + 1) * width] = acc[pl.ds(2 * s + j, 1)][0] + other[j]

    def drain(c):
        send_own(c, True)
        send_far(c, True)
        for k in (1, 2, 3):
            plane_step(k, c, True)
        for u in range(3):
            line_step(u, c, True)
    over(drain)


def fused(snapshots, slot_map, row_weight, valid_rows):
    rows, width = snapshots.shape
    sources = valid_rows.shape[1]
    kept = (sources - 1) * (rows // sources)
    panel = (4, CHUNKS, width // CHUNKS, kept)
    full = 4 * width
    dma = pltpu.SemaphoreType.DMA
    grid4 = dma((4, CHUNKS))
    return pl.pallas_call(
        gram_kernel,
        out_shape=jax.ShapeDtypeStruct((2 * width, full), jnp.float32),
        in_specs=[
            pl.BlockSpec(memory_space=pltpu.VMEM),
            pl.BlockSpec(memory_space=pltpu.VMEM),
            pl.BlockSpec(memory_space=pltpu.VMEM),
            pl.BlockSpec(memory_space=pltpu.SMEM),
        ],
        out_specs=pl.BlockSpec(memory_space=pltpu.VMEM),
        scratch_shapes=[
            pltpu.VMEM(panel, jnp.bfloat16),
            pltpu.VMEM(panel, jnp.bfloat16),
            pltpu.VMEM(panel, jnp.bfloat16),
            pltpu.VMEM((1, kept), jnp.float32),
            pltpu.VMEM((4, width, full), jnp.float32),
            pltpu.VMEM((2, width, full), jnp.float32),
            dma((1,)), grid4, grid4, grid4, grid4, grid4, grid4, grid4, dma((2,)), dma((2,)),
        ],
        compiler_params=pltpu.CompilerParams(
            collective_id=0, has_side_effects=True, vmem_limit_bytes=40 * 2**20
        ),
        cost_estimate=pl.CostEstimate(
            flops=2 * full * full * kept, bytes_accessed=8 * 2**20, transcendentals=0
        ),
    )(snapshots, slot_map, row_weight, valid_rows)


def solution(mesh):
    shape = dict(mesh.shape)
    use_kernel = shape == {"bi": 4, "bj": 4, "sl": 2}
    return jax.shard_map(
        fused if use_kernel else body,
        mesh=mesh,
        in_specs=(P("sl", ("bj", "bi")), P(("bj", "bi"), None), P("sl"), P("sl", None)),
        out_specs=P(("bi", "sl"), "bj"),
        check_vma=False,
    )
```

```python
import jax
import jax.numpy as jnp
from jax import lax
from jax.experimental import pallas as pl
from jax.experimental.pallas import tpu as pltpu
from jax.sharding import PartitionSpec as P

MESH = pl.DeviceIdType.MESH
CHUNKS = 4


def nt(a, b):
    return lax.dot_general(a, b, (((1,), (1,)), ((), ())), preferred_element_type=jnp.float32)


def contract_rows(left_panel, right_panel):
    return lax.dot_general(
        left_panel, right_panel, (((0,), (0,)), ((), ())), preferred_element_type=jnp.float32
    )


def body(snapshots, slot_map, row_weight, valid_rows):
    local_rows = snapshots.shape[0]
    sources_here = valid_rows.shape[1]
    source_rows = local_rows // sources_here
    ordered = jnp.zeros_like(snapshots).at[:, slot_map[0]].set(snapshots)
    positions = jnp.arange(local_rows, dtype=jnp.int32)
    source = positions // source_rows
    within = positions % source_rows
    source_ids = jnp.arange(sources_here, dtype=jnp.int32)
    matches = source[:, None] == source_ids[None, :]
    row_limit = jnp.sum(jnp.where(matches, valid_rows[0][None, :], 0), axis=1)
    row_factor = jnp.where(within < row_limit, row_weight, jnp.zeros_like(row_weight))
    count_bi = lax.axis_size("bi")
    count_bj = lax.axis_size("bj")
    per_row = count_bj // count_bi
    row_count = ordered.shape[0]
    shard_width = ordered.shape[1]
    column_panel = lax.all_gather(ordered, "bi", axis=1, tiled=True)
    weighted_shard = (ordered.astype(jnp.float32) * row_factor[:, None]).astype(jnp.bfloat16)
    sectioned = weighted_shard.reshape(row_count, 1, 1, shard_width)
    moved = lax.all_to_all(
        lax.all_to_all(sectioned, "bj", split_axis=0, concat_axis=1, tiled=True),
        "bi",
        split_axis=1,
        concat_axis=2,
        tiled=True,
    )
    gathered = lax.all_gather(moved, "bj", axis=0, tiled=True)
    weighted = gathered.reshape(row_count, per_row * count_bi * shard_width)
    return lax.psum_scatter(
        contract_rows(weighted, column_panel), "sl", scatter_dimension=0, tiled=True
    )


def gram_kernel(
    snap_in, slot_in, weight_in, valid_in, out,
    snap, slot, weight, valid, insem, colp, rowp, offl, wrow, acc, other,
    own_z, gsend, grecv, upsend, dnsend, rrecv, orecv, psend, ssend, srecv,
):
    r = lax.axis_index("bi")
    z = lax.axis_index("bj")
    s = lax.axis_index("sl")
    width, rows = snap.shape
    sources = valid.shape[1]
    src_rows = rows // sources
    kept = (sources - 1) * src_rows
    C = CHUNKS
    part = width // C
    diag = r == z
    not_diag = r != z
    low = z > 0
    high = z < 3

    loads = [
        pltpu.make_async_copy(src, dst, insem.at[i])
        for i, (src, dst) in enumerate(
            ((snap_in, snap), (slot_in, slot), (valid_in, valid), (weight_in, weight)))
    ]
    for load in loads:
        load.start()
    barrier = pltpu.get_barrier_semaphore()
    for k in (1, 2, 3):
        mate = (r + k) % 4
        pl.semaphore_signal(barrier, inc=1, device_id={"bi": mate}, device_id_type=MESH)
    pl.semaphore_signal(barrier, inc=1, device_id={"sl": 1 - s}, device_id_type=MESH)

    @pl.when(low)
    def _():
        pl.semaphore_signal(barrier, inc=1, device_id={"bj": z - 1}, device_id_type=MESH)

    @pl.when(high)
    def _():
        pl.semaphore_signal(barrier, inc=1, device_id={"bj": z + 1}, device_id_type=MESH)

    for load in loads:
        load.wait()
    place = lax.broadcasted_iota(jnp.int32, (width, width), 0)
    turn = (place == slot[...]).astype(jnp.float32).astype(jnp.bfloat16)
    turned = jnp.dot(turn, snap[...], preferred_element_type=jnp.float32).astype(jnp.bfloat16)
    start = jnp.int32(0)
    targets = []
    lane = lax.broadcasted_iota(jnp.int32, (1, src_rows), 1)
    for q in range(sources):
        count = valid[0, q]
        targets.append(jnp.where(lane < count, lane + start, -1))
        start = start + count
    target = jnp.concatenate(targets, axis=1)
    choose = (lax.broadcasted_iota(jnp.int32, (kept, rows), 0) == target)
    choose = choose.astype(jnp.float32).astype(jnp.bfloat16)
    w = weight[...].reshape(1, rows)
    hi = w.astype(jnp.bfloat16).astype(jnp.float32)
    mid = (w - hi).astype(jnp.bfloat16).astype(jnp.float32)
    low_bits = w - hi - mid
    pieces = jnp.concatenate([hi, mid, low_bits, jnp.zeros((13, rows), jnp.float32)], axis=0)
    packed = nt(jnp.concatenate([turned, pieces.astype(jnp.bfloat16)], axis=0), choose)
    colp[pl.ds(r, 1)] = packed[:width].astype(jnp.bfloat16).reshape(1, C, part, kept)
    wrow[...] = packed[width:width + 1] + packed[width + 1:width + 2] + packed[width + 2:width + 3]

    pl.semaphore_wait(barrier, 4 + (z + 3) // 4 + (6 - z) // 4)

    def to_plane(k, c):
        return pltpu.make_async_remote_copy(
            src_ref=colp.at[r, c], dst_ref=colp.at[r, c],
            send_sem=gsend.at[k, c], recv_sem=grecv.at[r, c],
            device_id={"bi": flip(k)}, device_id_type=MESH)

    def flip(k):
        x, y = r % 2, r // 2
        x = 1 - x if k % 2 else x
        y = 1 - y if k // 2 else y
        return 2 * y + x

    def along(src, dst, step, sends, recvs, b, c):
        return pltpu.make_async_remote_copy(
            src_ref=src.at[b, c], dst_ref=dst.at[b, c],
            send_sem=sends.at[b, c], recv_sem=recvs.at[b, c],
            device_id={"bj": z + step}, device_id_type=MESH)

    def up_row(src, b, c):
        return along(src, rowp, 1, upsend, rrecv, b, c)

    def dn_row(src, b, c):
        return along(src, rowp, -1, dnsend, rrecv, b, c)

    def own_off(step, sends, c):
        return pltpu.make_async_remote_copy(
            src_ref=colp.at[r, c], dst_ref=offl.at[z, c],
            send_sem=sends.at[z, c], recv_sem=orecv.at[z, c],
            device_id={"bj": z + step}, device_id_type=MESH)

    def hand(p, c):
        return pltpu.make_async_remote_copy(
            src_ref=offl.at[p, c], dst_ref=rowp.at[r, c],
            send_sem=psend.at[p, c], recv_sem=rrecv.at[r, c],
            device_id={"bi": p}, device_id_type=MESH)

    def got(buf, recvs, b, c):
        pltpu.make_async_remote_copy(
            src_ref=buf.at[b, c], dst_ref=buf.at[b, c],
            send_sem=own_z.at[0], recv_sem=recvs.at[b, c],
            device_id={"sl": 1 - s}, device_id_type=MESH).wait_recv()

    def act(condition, copy, drain):
        @pl.when(condition)
        def _():
            if drain:
                copy().wait_send()
            else:
                copy().start()

    down = (r - z + 3 + r // 3) // 4
    second = down * (3 - r // 3) + (1 - down) * (1 - (r + 2) // 3)
    third = down * 6 + (1 - down) * 3 - r - second
    lent = (1 - down) * 3
    natural = (r, second, third)
    off_down = (r == 0)
    off_up = (r == 3)

    def send_own(c, drain):
        act(diag & low, lambda: dn_row(colp, r, c), drain)
        act(diag & high, lambda: up_row(colp, r, c), drain)
        act(off_down & low, lambda: own_off(-1, dnsend, c), drain)
        act(off_up & high, lambda: own_off(1, upsend, c), drain)
        for k in (1, 2):
            act(r >= 0, lambda: to_plane(k, c), drain)

    def relay(k, c):
        b = flip(k)
        return pltpu.make_async_remote_copy(
            src_ref=colp.at[b, c], dst_ref=colp.at[b, c],
            send_sem=gsend.at[3, c], recv_sem=grecv.at[b, c],
            device_id={"bi": flip(3 - k)}, device_id_type=MESH)

    def plane_step(k, c, drain):
        b = flip(k)
        if not drain:
            got(colp, grecv, b, c)
        if k != 3:
            act(c % 2 == k - 1, lambda: relay(k, c), drain)
        act(diag & low & (b >= 1), lambda: dn_row(colp, b, c), drain)
        act(diag & high & (b <= 2), lambda: up_row(colp, b, c), drain)

    def line_step(u, c, drain):
        p_dn = z + 1 + u

        @pl.when(off_down & (p_dn <= 3))
        def _():
            if not drain:
                got(offl, orecv, p_dn, c)
            act(low, lambda: along(offl, offl, -1, dnsend, orecv, p_dn, c), drain)
            act(r >= 0, lambda: hand(p_dn, c), drain)

        p_up = z - 1 - u

        @pl.when(off_up & (p_up >= 0))
        def _():
            if not drain:
                got(offl, orecv, p_up, c)
            act(high, lambda: along(offl, offl, 1, upsend, orecv, p_up, c), drain)
            act(r >= 0, lambda: hand(p_up, c), drain)

        b = natural[u]

        @pl.when(not_diag)
        def _():
            if not drain:
                got(rowp, rrecv, b, c)
        act((z < r) & low, lambda: dn_row(rowp, b, c), drain)
        act((z > r) & high, lambda: up_row(rowp, b, c), drain)

    def over(step):
        def one(c, carry):
            step(c)
            return carry
        lax.fori_loop(0, C, one, 0)

    def to_sister(b):
        return pltpu.make_async_remote_copy(
            src_ref=acc.at[b], dst_ref=other.at[b % 2],
            send_sem=ssend.at[b % 2], recv_sem=srecv.at[b % 2],
            device_id={"sl": 1 - s}, device_id_type=MESH)

    def multiply(b):
        @pl.when(diag)
        def _():
            rowp[pl.ds(b, 1)] = colp[pl.ds(b, 1)]
        block = rowp[pl.ds(b, 1)].reshape(width, kept).astype(jnp.float32)
        weighted = (block * wrow[...]).astype(jnp.bfloat16)
        acc[pl.ds(b, 1)] = nt(weighted, colp[...].reshape(4 * width, kept))[None]

        @pl.when(b // 2 != s)
        def _():
            to_sister(b).start()

    over(lambda c: send_own(c, False))

    def first(c):
        plane_step(1, c, False)
        plane_step(2, c, False)
        line_step(0, c, False)
    over(first)

    @pl.when(diag)
    def _():
        over(lambda c: plane_step(3, c, False))
    over(lambda c: line_step(1, c, False))

    @pl.when(not_diag)
    def _():
        over(lambda c: plane_step(3, c, False))
    multiply(natural[0])
    multiply(natural[1])
    over(lambda c: line_step(2, c, False))
    multiply(natural[2])

    def last(c):
        @pl.when(not_diag)
        def _():
            got(rowp, rrecv, lent, c)
    over(last)
    multiply(lent)

    for j in range(2):
        pltpu.make_async_remote_copy(
            src_ref=acc.at[j], dst_ref=other.at[j], send_sem=ssend.at[j], recv_sem=srecv.at[j],
            device_id={"sl": 1 - s}, device_id_type=MESH).wait()
        out[j * width:(j + 1) * width] = acc[pl.ds(2 * s + j, 1)][0] + other[j]

    def drain(c):
        send_own(c, True)
        for k in (1, 2, 3):
            plane_step(k, c, True)
        for u in range(3):
            line_step(u, c, True)
    over(drain)


def fused(snapshots, slot_map, row_weight, valid_rows):
    rows, width = snapshots.shape
    sources = valid_rows.shape[1]
    hbm = pl.BlockSpec(memory_space=pltpu.HBM)
    kept = (sources - 1) * (rows // sources)
    panel = (4, CHUNKS, width // CHUNKS, kept)
    full = 4 * width
    dma = pltpu.SemaphoreType.DMA
    grid4 = dma((4, CHUNKS))
    return pl.pallas_call(
        gram_kernel,
        out_shape=jax.ShapeDtypeStruct((2 * width, full), jnp.float32),
        in_specs=[hbm] * 4,
        out_specs=pl.BlockSpec(memory_space=pltpu.VMEM),
        scratch_shapes=[
            pltpu.VMEM((width, rows), jnp.bfloat16),
            pltpu.VMEM(slot_map.shape, jnp.int32),
            pltpu.VMEM(row_weight.shape, jnp.float32),
            pltpu.SMEM(valid_rows.shape, jnp.int32),
            dma((4,)),
            pltpu.VMEM(panel, jnp.bfloat16),
            pltpu.VMEM(panel, jnp.bfloat16),
            pltpu.VMEM(panel, jnp.bfloat16),
            pltpu.VMEM((1, kept), jnp.float32),
            pltpu.VMEM((4, width, full), jnp.float32),
            pltpu.VMEM((2, width, full), jnp.float32),
            dma((1,)), grid4, grid4, grid4, grid4, grid4, grid4, grid4, dma((2,)), dma((2,)),
        ],
        compiler_params=pltpu.CompilerParams(
            collective_id=0, has_side_effects=True, vmem_limit_bytes=63 * 2**20
        ),
        cost_estimate=pl.CostEstimate(
            flops=2 * full * full * kept, bytes_accessed=8 * 2**20, transcendentals=0
        ),
    )(snapshots.T, slot_map, row_weight, valid_rows)


def solution(mesh):
    shape = dict(mesh.shape)
    use_kernel = shape == {"bi": 4, "bj": 4, "sl": 2}
    return jax.shard_map(
        fused if use_kernel else body,
        mesh=mesh,
        in_specs=(P("sl", ("bj", "bi")), P(("bj", "bi"), None), P("sl"), P("sl", None)),
        out_specs=P(("bi", "sl"), "bj"),
        check_vma=False,
    )
```

```python
import jax
import jax.numpy as jnp
from jax import lax
from jax.experimental import pallas as pl
from jax.experimental.pallas import tpu as pltpu
from jax.sharding import PartitionSpec as P

MESH = pl.DeviceIdType.MESH
CHUNKS = 6


def nt(a, b):
    return lax.dot_general(a, b, (((1,), (1,)), ((), ())), preferred_element_type=jnp.float32)


def contract_rows(left_panel, right_panel):
    return lax.dot_general(
        left_panel, right_panel, (((0,), (0,)), ((), ())), preferred_element_type=jnp.float32
    )


def body(snapshots, slot_map, row_weight, valid_rows):
    local_rows = snapshots.shape[0]
    sources_here = valid_rows.shape[1]
    source_rows = local_rows // sources_here
    ordered = jnp.zeros_like(snapshots).at[:, slot_map[0]].set(snapshots)
    positions = jnp.arange(local_rows, dtype=jnp.int32)
    source = positions // source_rows
    within = positions % source_rows
    source_ids = jnp.arange(sources_here, dtype=jnp.int32)
    matches = source[:, None] == source_ids[None, :]
    row_limit = jnp.sum(jnp.where(matches, valid_rows[0][None, :], 0), axis=1)
    row_factor = jnp.where(within < row_limit, row_weight, jnp.zeros_like(row_weight))
    count_bi = lax.axis_size("bi")
    count_bj = lax.axis_size("bj")
    per_row = count_bj // count_bi
    row_count = ordered.shape[0]
    shard_width = ordered.shape[1]
    column_panel = lax.all_gather(ordered, "bi", axis=1, tiled=True)
    weighted_shard = (ordered.astype(jnp.float32) * row_factor[:, None]).astype(jnp.bfloat16)
    sectioned = weighted_shard.reshape(row_count, 1, 1, shard_width)
    moved = lax.all_to_all(
        lax.all_to_all(sectioned, "bj", split_axis=0, concat_axis=1, tiled=True),
        "bi",
        split_axis=1,
        concat_axis=2,
        tiled=True,
    )
    gathered = lax.all_gather(moved, "bj", axis=0, tiled=True)
    weighted = gathered.reshape(row_count, per_row * count_bi * shard_width)
    return lax.psum_scatter(
        contract_rows(weighted, column_panel), "sl", scatter_dimension=0, tiled=True
    )


def gram_kernel(
    snap_in, slot_in, weight_in, valid_in, mine, other,
    snap, slot, weight, valid, insem, colp, rowp, offl, wrow, acc,
    own_z, gsend, grecv, upsend, dnsend, rrecv, orecv, psend, ssend, srecv, ksem,
):
    r = lax.axis_index("bi")
    z = lax.axis_index("bj")
    s = lax.axis_index("sl")
    width, rows = snap.shape
    sources = valid.shape[1]
    src_rows = rows // sources
    kept = (sources - 1) * src_rows
    C = CHUNKS
    part = width // C
    diag = r == z
    not_diag = r != z
    low = z > 0
    high = z < 3

    loads = [
        pltpu.make_async_copy(src, dst, insem.at[i])
        for i, (src, dst) in enumerate(
            ((snap_in, snap), (slot_in, slot), (valid_in, valid), (weight_in, weight)))
    ]
    for load in loads:
        load.start()
    barrier = pltpu.get_barrier_semaphore()
    for k in (1, 2, 3):
        mate = (r + k) % 4
        pl.semaphore_signal(barrier, inc=1, device_id={"bi": mate}, device_id_type=MESH)
    pl.semaphore_signal(barrier, inc=1, device_id={"sl": 1 - s}, device_id_type=MESH)

    @pl.when(low)
    def _():
        pl.semaphore_signal(barrier, inc=1, device_id={"bj": z - 1}, device_id_type=MESH)

    @pl.when(high)
    def _():
        pl.semaphore_signal(barrier, inc=1, device_id={"bj": z + 1}, device_id_type=MESH)

    for load in loads:
        load.wait()
    place = lax.broadcasted_iota(jnp.int32, (width, width), 0)
    turn = (place == slot[...]).astype(jnp.float32).astype(jnp.bfloat16)
    turned = jnp.dot(turn, snap[...], preferred_element_type=jnp.float32).astype(jnp.bfloat16)
    start = jnp.int32(0)
    targets = []
    lane = lax.broadcasted_iota(jnp.int32, (1, src_rows), 1)
    for q in range(sources):
        count = valid[0, q]
        targets.append(jnp.where(lane < count, lane + start, -1))
        start = start + count
    target = jnp.concatenate(targets, axis=1)
    choose = (lax.broadcasted_iota(jnp.int32, (kept, rows), 0) == target)
    choose = choose.astype(jnp.float32).astype(jnp.bfloat16)
    w = weight[...].reshape(1, rows)
    hi = w.astype(jnp.bfloat16).astype(jnp.float32)
    mid = (w - hi).astype(jnp.bfloat16).astype(jnp.float32)
    low_bits = w - hi - mid
    pieces = jnp.concatenate([hi, mid, low_bits, jnp.zeros((13, rows), jnp.float32)], axis=0)
    packed = nt(jnp.concatenate([turned, pieces.astype(jnp.bfloat16)], axis=0), choose)
    colp[pl.ds(r, 1)] = packed[:width].astype(jnp.bfloat16).reshape(1, C, part, kept)
    wrow[...] = packed[width:width + 1] + packed[width + 1:width + 2] + packed[width + 2:width + 3]

    pl.semaphore_wait(barrier, 4 + (z + 3) // 4 + (6 - z) // 4)

    def to_plane(k, c):
        return pltpu.make_async_remote_copy(
            src_ref=colp.at[r, c], dst_ref=colp.at[r, c],
            send_sem=gsend.at[k, c], recv_sem=grecv.at[r, c],
            device_id={"bi": flip(k)}, device_id_type=MESH)

    def flip(k):
        x, y = r % 2, r // 2
        x = 1 - x if k % 2 else x
        y = 1 - y if k // 2 else y
        return 2 * y + x

    def along(src, dst, step, sends, recvs, b, c):
        return pltpu.make_async_remote_copy(
            src_ref=src.at[b, c], dst_ref=dst.at[b, c],
            send_sem=sends.at[b, c], recv_sem=recvs.at[b, c],
            device_id={"bj": z + step}, device_id_type=MESH)

    def up_row(src, b, c):
        return along(src, rowp, 1, upsend, rrecv, b, c)

    def dn_row(src, b, c):
        return along(src, rowp, -1, dnsend, rrecv, b, c)

    def own_off(step, sends, c):
        return pltpu.make_async_remote_copy(
            src_ref=colp.at[r, c], dst_ref=offl.at[z, c],
            send_sem=sends.at[z, c], recv_sem=orecv.at[z, c],
            device_id={"bj": z + step}, device_id_type=MESH)

    def hand(p, c):
        return pltpu.make_async_remote_copy(
            src_ref=offl.at[p, c], dst_ref=rowp.at[r, c],
            send_sem=psend.at[p, c], recv_sem=rrecv.at[r, c],
            device_id={"bi": p}, device_id_type=MESH)

    def got(buf, recvs, b, c):
        pltpu.make_async_remote_copy(
            src_ref=buf.at[b, c], dst_ref=buf.at[b, c],
            send_sem=own_z.at[0], recv_sem=recvs.at[b, c],
            device_id={"sl": 1 - s}, device_id_type=MESH).wait_recv()

    def act(condition, copy, drain):
        @pl.when(condition)
        def _():
            if drain:
                copy().wait_send()
            else:
                copy().start()

    down = (r - z + 3 + r // 3) // 4
    second = down * (3 - r // 3) + (1 - down) * (1 - (r + 2) // 3)
    third = down * 6 + (1 - down) * 3 - r - second
    lent = (1 - down) * 3
    natural = (r, second, third)
    off_down = (r == 0)
    off_up = (r == 3)

    def send_own(c, drain):
        act(diag & low, lambda: dn_row(colp, r, c), drain)
        act(diag & high, lambda: up_row(colp, r, c), drain)
        act(off_down & low, lambda: own_off(-1, dnsend, c), drain)
        act(off_up & high, lambda: own_off(1, upsend, c), drain)
        for k in (1, 2):
            act(r >= 0, lambda: to_plane(k, c), drain)

    def relay(k, c):
        b = flip(k)
        return pltpu.make_async_remote_copy(
            src_ref=colp.at[b, c], dst_ref=colp.at[b, c],
            send_sem=gsend.at[3, c], recv_sem=grecv.at[b, c],
            device_id={"bi": flip(3 - k)}, device_id_type=MESH)

    def plane_step(k, c, drain):
        b = flip(k)
        if not drain:
            got(colp, grecv, b, c)
        if k != 3:
            act(c % 2 == k - 1, lambda: relay(k, c), drain)
        act(diag & low & (b >= 1), lambda: dn_row(colp, b, c), drain)
        act(diag & high & (b <= 2), lambda: up_row(colp, b, c), drain)

    def line_step(u, c, drain):
        p_dn = z + 1 + u

        @pl.when(off_down & (p_dn <= 3))
        def _():
            if not drain:
                got(offl, orecv, p_dn, c)
            act(low, lambda: along(offl, offl, -1, dnsend, orecv, p_dn, c), drain)
            act(r >= 0, lambda: hand(p_dn, c), drain)

        p_up = z - 1 - u

        @pl.when(off_up & (p_up >= 0))
        def _():
            if not drain:
                got(offl, orecv, p_up, c)
            act(high, lambda: along(offl, offl, 1, upsend, orecv, p_up, c), drain)
            act(r >= 0, lambda: hand(p_up, c), drain)

        b = natural[u]

        @pl.when(not_diag)
        def _():
            if not drain:
                got(rowp, rrecv, b, c)
        act((z < r) & low, lambda: dn_row(rowp, b, c), drain)
        act((z > r) & high, lambda: up_row(rowp, b, c), drain)

    def over(step):
        def one(c, carry):
            step(c)
            return carry
        lax.fori_loop(0, C, one, 0)

    def to_sister(b):
        return pltpu.make_async_remote_copy(
            src_ref=acc.at[b], dst_ref=other.at[b % 2],
            send_sem=ssend.at[b % 2], recv_sem=srecv.at[b % 2],
            device_id={"sl": 1 - s}, device_id_type=MESH)

    def keep(b):
        return pltpu.make_async_copy(acc.at[b], mine.at[b % 2], ksem.at[b % 2])

    def multiply(b):
        @pl.when(diag)
        def _():
            rowp[pl.ds(b, 1)] = colp[pl.ds(b, 1)]
        block = rowp[pl.ds(b, 1)].reshape(width, kept).astype(jnp.float32)
        weighted = (block * wrow[...]).astype(jnp.bfloat16)
        acc[pl.ds(b, 1)] = nt(weighted, colp[...].reshape(4 * width, kept))[None]

        @pl.when(b // 2 != s)
        def _():
            to_sister(b).start()

        @pl.when(b // 2 == s)
        def _():
            keep(b).start()

    over(lambda c: send_own(c, False))

    def first(c):
        plane_step(1, c, False)
        plane_step(2, c, False)
        line_step(0, c, False)
    over(first)

    @pl.when(diag)
    def _():
        over(lambda c: plane_step(3, c, False))
    over(lambda c: line_step(1, c, False))

    def two():
        @pl.when(not_diag)
        def _():
            over(lambda c: plane_step(3, c, False))

        def one(i, carry):
            multiply(natural[0] * (1 - i) + natural[1] * i)
            return carry
        lax.fori_loop(0, 2, one, 0)

    is_end = ((z == 0) & (r >= 1)) | ((z == 3) & (r <= 2))
    pl.when(is_end)(two)
    over(lambda c: line_step(2, c, False))
    pl.when(jnp.logical_not(is_end))(two)
    multiply(natural[2])

    def last(c):
        @pl.when(not_diag)
        def _():
            got(rowp, rrecv, lent, c)
    over(last)
    multiply(lent)

    for j in range(2):
        pltpu.make_async_remote_copy(
            src_ref=acc.at[j], dst_ref=other.at[j], send_sem=ssend.at[j], recv_sem=srecv.at[j],
            device_id={"sl": 1 - s}, device_id_type=MESH).wait()
        keep(2 * s + j).wait()

    def drain(c):
        send_own(c, True)
        for k in (1, 2, 3):
            plane_step(k, c, True)
        for u in range(3):
            line_step(u, c, True)
    over(drain)


def fused(snapshots, slot_map, row_weight, valid_rows):
    rows, width = snapshots.shape
    sources = valid_rows.shape[1]
    hbm = pl.BlockSpec(memory_space=pltpu.HBM)
    kept = (sources - 1) * (rows // sources)
    panel = (4, CHUNKS, width // CHUNKS, kept)
    full = 4 * width
    dma = pltpu.SemaphoreType.DMA
    grid4 = dma((4, CHUNKS))
    half = jax.ShapeDtypeStruct((2, width, full), jnp.float32)
    mine, other = pl.pallas_call(
        gram_kernel,
        out_shape=(half, half),
        in_specs=[hbm] * 4,
        out_specs=(hbm, hbm),
        scratch_shapes=[
            pltpu.VMEM((width, rows), jnp.bfloat16),
            pltpu.VMEM(slot_map.shape, jnp.int32),
            pltpu.VMEM(row_weight.shape, jnp.float32),
            pltpu.SMEM(valid_rows.shape, jnp.int32),
            dma((4,)),
            pltpu.VMEM(panel, jnp.bfloat16),
            pltpu.VMEM(panel, jnp.bfloat16),
            pltpu.VMEM(panel, jnp.bfloat16),
            pltpu.VMEM((1, kept), jnp.float32),
            pltpu.VMEM((4, width, full), jnp.float32),
            dma((1,)), grid4, grid4, grid4, grid4, grid4, grid4, grid4, dma((2,)), dma((2,)), dma((2,)),
        ],
        compiler_params=pltpu.CompilerParams(
            collective_id=0, has_side_effects=True, vmem_limit_bytes=63 * 2**20
        ),
        cost_estimate=pl.CostEstimate(
            flops=2 * full * full * kept, bytes_accessed=8 * 2**20, transcendentals=0
        ),
    )(snapshots.T, slot_map, row_weight, valid_rows)
    return (mine + other).reshape(2 * width, full)


def solution(mesh):
    shape = dict(mesh.shape)
    use_kernel = shape == {"bi": 4, "bj": 4, "sl": 2}
    return jax.shard_map(
        fused if use_kernel else body,
        mesh=mesh,
        in_specs=(P("sl", ("bj", "bi")), P(("bj", "bi"), None), P("sl"), P("sl", None)),
        out_specs=P(("bi", "sl"), "bj"),
        check_vma=False,
    )
```

```python
import jax
import jax.numpy as jnp
from jax import lax
from jax.experimental import pallas as pl
from jax.experimental.pallas import tpu as pltpu
from jax.sharding import PartitionSpec as P

MESH = pl.DeviceIdType.MESH
CHUNKS = 3
LENT = 3


def nt(a, b):
    return lax.dot_general(a, b, (((1,), (1,)), ((), ())), preferred_element_type=jnp.float32)


def contract_rows(left_panel, right_panel):
    return lax.dot_general(
        left_panel, right_panel, (((0,), (0,)), ((), ())), preferred_element_type=jnp.float32
    )


def body(snapshots, slot_map, row_weight, valid_rows):
    local_rows = snapshots.shape[0]
    sources_here = valid_rows.shape[1]
    source_rows = local_rows // sources_here
    ordered = jnp.zeros_like(snapshots).at[:, slot_map[0]].set(snapshots)
    positions = jnp.arange(local_rows, dtype=jnp.int32)
    source = positions // source_rows
    within = positions % source_rows
    source_ids = jnp.arange(sources_here, dtype=jnp.int32)
    matches = source[:, None] == source_ids[None, :]
    row_limit = jnp.sum(jnp.where(matches, valid_rows[0][None, :], 0), axis=1)
    row_factor = jnp.where(within < row_limit, row_weight, jnp.zeros_like(row_weight))
    count_bi = lax.axis_size("bi")
    count_bj = lax.axis_size("bj")
    per_row = count_bj // count_bi
    row_count = ordered.shape[0]
    shard_width = ordered.shape[1]
    column_panel = lax.all_gather(ordered, "bi", axis=1, tiled=True)
    weighted_shard = (ordered.astype(jnp.float32) * row_factor[:, None]).astype(jnp.bfloat16)
    sectioned = weighted_shard.reshape(row_count, 1, 1, shard_width)
    moved = lax.all_to_all(
        lax.all_to_all(sectioned, "bj", split_axis=0, concat_axis=1, tiled=True),
        "bi",
        split_axis=1,
        concat_axis=2,
        tiled=True,
    )
    gathered = lax.all_gather(moved, "bj", axis=0, tiled=True)
    weighted = gathered.reshape(row_count, per_row * count_bi * shard_width)
    return lax.psum_scatter(
        contract_rows(weighted, column_panel), "sl", scatter_dimension=0, tiled=True
    )


def gram_kernel(
    snap_in, slot_in, weight_in, valid_in, mine, other,
    snap, slot, weight, valid, insem, colp, rowp, offl, wrow, acc,
    own_z, gsend, grecv, upsend, dnsend, rrecv, orecv, psend, ssend, srecv, ksem,
):
    r = lax.axis_index("bi")
    z = lax.axis_index("bj")
    s = lax.axis_index("sl")
    width, rows = snap.shape
    sources = valid.shape[1]
    src_rows = rows // sources
    kept = (sources - 1) * src_rows
    C = CHUNKS
    part = width // C
    diag = r == z
    not_diag = r != z
    low = z > 0
    high = z < 3

    loads = [
        pltpu.make_async_copy(src, dst, insem.at[i])
        for i, (src, dst) in enumerate(
            ((snap_in, snap), (slot_in, slot), (valid_in, valid), (weight_in, weight)))
    ]
    for load in loads:
        load.start()
    barrier = pltpu.get_barrier_semaphore()
    for k in (1, 2, 3):
        mate = (r + k) % 4
        pl.semaphore_signal(barrier, inc=1, device_id={"bi": mate}, device_id_type=MESH)
    pl.semaphore_signal(barrier, inc=1, device_id={"sl": 1 - s}, device_id_type=MESH)

    @pl.when(low)
    def _():
        pl.semaphore_signal(barrier, inc=1, device_id={"bj": z - 1}, device_id_type=MESH)

    @pl.when(high)
    def _():
        pl.semaphore_signal(barrier, inc=1, device_id={"bj": z + 1}, device_id_type=MESH)

    for load in loads:
        load.wait()
    place = lax.broadcasted_iota(jnp.int32, (width, width), 0)
    turn = (place == slot[...]).astype(jnp.float32).astype(jnp.bfloat16)
    turned = jnp.dot(turn, snap[...], preferred_element_type=jnp.float32).astype(jnp.bfloat16)
    start = jnp.int32(0)
    targets = []
    lane = lax.broadcasted_iota(jnp.int32, (1, src_rows), 1)
    for q in range(sources):
        count = valid[0, q]
        targets.append(jnp.where(lane < count, lane + start, -1))
        start = start + count
    target = jnp.concatenate(targets, axis=1)
    choose = (lax.broadcasted_iota(jnp.int32, (kept, rows), 0) == target)
    choose = choose.astype(jnp.float32).astype(jnp.bfloat16)
    w = weight[...].reshape(1, rows)
    hi = w.astype(jnp.bfloat16).astype(jnp.float32)
    mid = (w - hi).astype(jnp.bfloat16).astype(jnp.float32)
    low_bits = w - hi - mid
    pieces = jnp.concatenate([hi, mid, low_bits, jnp.zeros((13, rows), jnp.float32)], axis=0)
    packed = nt(jnp.concatenate([turned, pieces.astype(jnp.bfloat16)], axis=0), choose)
    colp[pl.ds(r, 1)] = packed[:width].astype(jnp.bfloat16).reshape(1, C, part, kept)
    wrow[...] = packed[width:width + 1] + packed[width + 1:width + 2] + packed[width + 2:width + 3]

    pl.semaphore_wait(barrier, 4 + (z + 3) // 4 + (6 - z) // 4)

    def to_plane(k, c):
        return pltpu.make_async_remote_copy(
            src_ref=colp.at[r, c], dst_ref=colp.at[r, c],
            send_sem=gsend.at[k, c], recv_sem=grecv.at[r, c],
            device_id={"bi": flip(k)}, device_id_type=MESH)

    def flip(k):
        x, y = r % 2, r // 2
        x = 1 - x if k % 2 else x
        y = 1 - y if k // 2 else y
        return 2 * y + x

    def along(src, dst, step, sends, recvs, b, c):
        return pltpu.make_async_remote_copy(
            src_ref=src.at[b, c], dst_ref=dst.at[b, c],
            send_sem=sends.at[b, c], recv_sem=recvs.at[b, c],
            device_id={"bj": z + step}, device_id_type=MESH)

    def up_row(src, b, c):
        return along(src, rowp, 1, upsend, rrecv, b, c)

    def dn_row(src, b, c):
        return along(src, rowp, -1, dnsend, rrecv, b, c)

    def own_off(step, sends, c):
        return pltpu.make_async_remote_copy(
            src_ref=colp.at[r, c], dst_ref=offl.at[z, c],
            send_sem=sends.at[z, c], recv_sem=orecv.at[z, c],
            device_id={"bj": z + step}, device_id_type=MESH)

    def hand(p, c):
        return pltpu.make_async_remote_copy(
            src_ref=offl.at[p, c], dst_ref=rowp.at[r, c],
            send_sem=psend.at[p, c], recv_sem=rrecv.at[r, c],
            device_id={"bi": p}, device_id_type=MESH)

    def got(buf, recvs, b, c):
        pltpu.make_async_remote_copy(
            src_ref=buf.at[b, c], dst_ref=buf.at[b, c],
            send_sem=own_z.at[0], recv_sem=recvs.at[b, c],
            device_id={"sl": 1 - s}, device_id_type=MESH).wait_recv()

    def act(condition, copy, drain):
        @pl.when(condition)
        def _():
            if drain:
                copy().wait_send()
            else:
                copy().start()

    down = (r - z + 3 + r // 3) // 4
    second = down * (3 - r // 3) + (1 - down) * (1 - (r + 2) // 3)
    third = down * 6 + (1 - down) * 3 - r - second
    lent = (1 - down) * 3
    natural = (r, second, third, lent)
    off_down = (r == 0)
    off_up = (r == 3)

    def send_own(c, drain):
        act(diag & low, lambda: dn_row(colp, r, c), drain)
        act(diag & high, lambda: up_row(colp, r, c), drain)
        act(off_down & low & (c < LENT), lambda: own_off(-1, dnsend, c), drain)
        act(off_up & high & (c < LENT), lambda: own_off(1, upsend, c), drain)
        for k in (1, 2):
            act(r >= 0, lambda: to_plane(k, c), drain)

    def relay(k, c):
        b = flip(k)
        return pltpu.make_async_remote_copy(
            src_ref=colp.at[b, c], dst_ref=colp.at[b, c],
            send_sem=gsend.at[3, c], recv_sem=grecv.at[b, c],
            device_id={"bi": flip(3 - k)}, device_id_type=MESH)

    def plane_step(k, c, drain):
        b = flip(k)
        if not drain:
            got(colp, grecv, b, c)
        if k != 3:
            act(c % 2 == k - 1, lambda: relay(k, c), drain)
        act(diag & low & ((b >= 1) | (c >= LENT)), lambda: dn_row(colp, b, c), drain)
        act(diag & high & ((b <= 2) | (c >= LENT)), lambda: up_row(colp, b, c), drain)

    def line_step(u, c, drain):
        p_dn = z + 1 + u

        @pl.when(off_down & (p_dn <= 3) & (c < LENT))
        def _():
            if not drain:
                got(offl, orecv, p_dn, c)
            act(low, lambda: along(offl, offl, -1, dnsend, orecv, p_dn, c), drain)
            act(r >= 0, lambda: hand(p_dn, c), drain)

        p_up = z - 1 - u

        @pl.when(off_up & (p_up >= 0) & (c < LENT))
        def _():
            if not drain:
                got(offl, orecv, p_up, c)
            act(high, lambda: along(offl, offl, 1, upsend, orecv, p_up, c), drain)
            act(r >= 0, lambda: hand(p_up, c), drain)

        natural_step(u, c, drain)

    def natural_step(u, c, drain):
        b = natural[u]

        @pl.when(not_diag)
        def _():
            if not drain:
                got(rowp, rrecv, b, c)
        act((z < r) & low, lambda: dn_row(rowp, b, c), drain)
        act((z > r) & high, lambda: up_row(rowp, b, c), drain)

    def over(step):
        def one(c, carry):
            step(c)
            return carry
        lax.fori_loop(0, C, one, 0)

    def to_sister(b):
        return pltpu.make_async_remote_copy(
            src_ref=acc.at[b], dst_ref=other.at[b % 2],
            send_sem=ssend.at[b % 2], recv_sem=srecv.at[b % 2],
            device_id={"sl": 1 - s}, device_id_type=MESH)

    def keep(b):
        return pltpu.make_async_copy(acc.at[b], mine.at[b % 2], ksem.at[b % 2])

    def multiply(b):
        @pl.when(diag)
        def _():
            rowp[pl.ds(b, 1)] = colp[pl.ds(b, 1)]
        block = rowp[pl.ds(b, 1)].reshape(width, kept).astype(jnp.float32)
        weighted = (block * wrow[...]).astype(jnp.bfloat16)
        acc[pl.ds(b, 1)] = nt(weighted, colp[...].reshape(4 * width, kept))[None]

        @pl.when(b // 2 != s)
        def _():
            to_sister(b).start()

        @pl.when(b // 2 == s)
        def _():
            keep(b).start()

    over(lambda c: send_own(c, False))

    def first(c):
        plane_step(1, c, False)
        plane_step(2, c, False)
        line_step(0, c, False)
    over(first)

    @pl.when(diag)
    def _():
        over(lambda c: plane_step(3, c, False))
    in_turn = (r == 0) | (r == 3)
    is_end = ((z == 0) & (r >= 1)) | ((z == 3) & (r <= 2))
    is_middle = jnp.logical_not(is_end)

    def far_block():
        @pl.when(not_diag)
        def _():
            over(lambda c: plane_step(3, c, False))

    def products(lo, hi):
        def one(i, carry):
            b = r + (i % 2) * (second - r) + (i // 2) * (third - r)
            multiply(b)
            return carry
        lax.fori_loop(lo, hi, one, 0)

    @pl.when(is_end & in_turn)
    def _():
        far_block()
        products(0, 1)

    @pl.when(in_turn)
    def _():
        def both(c):
            line_step(1, c, False)
            line_step(2, c, False)
        over(both)

    @pl.when(is_end & in_turn)
    def _():
        products(1, 3)

    @pl.when(jnp.logical_not(in_turn))
    def _():
        over(lambda c: line_step(1, c, False))

        @pl.when(is_end)
        def _():
            far_block()
            products(0, 2)
        over(lambda c: line_step(2, c, False))

        @pl.when(is_end)
        def _():
            products(2, 3)

    @pl.when(is_middle)
    def _():
        far_block()
        products(0, 3)

    def last(c):
        @pl.when(c >= LENT)
        def _():
            natural_step(3, c, False)

        @pl.when(not_diag & (c < LENT))
        def _():
            got(rowp, rrecv, lent, c)

    over(last)
    multiply(lent)

    for j in range(2):
        pltpu.make_async_remote_copy(
            src_ref=acc.at[j], dst_ref=other.at[j], send_sem=ssend.at[j], recv_sem=srecv.at[j],
            device_id={"sl": 1 - s}, device_id_type=MESH).wait()
        keep(2 * s + j).wait()

    def drain(c):
        send_own(c, True)
        for k in (1, 2, 3):
            plane_step(k, c, True)
        for u in range(3):
            line_step(u, c, True)

        @pl.when(c >= LENT)
        def _():
            natural_step(3, c, True)
    over(drain)


def fused(snapshots, slot_map, row_weight, valid_rows):
    rows, width = snapshots.shape
    sources = valid_rows.shape[1]
    hbm = pl.BlockSpec(memory_space=pltpu.HBM)
    kept = (sources - 1) * (rows // sources)
    panel = (4, CHUNKS, width // CHUNKS, kept)
    full = 4 * width
    dma = pltpu.SemaphoreType.DMA
    grid4 = dma((4, CHUNKS))
    half = jax.ShapeDtypeStruct((2, width, full), jnp.float32)
    mine, other = pl.pallas_call(
        gram_kernel,
        out_shape=(half, half),
        in_specs=[hbm] * 4,
        out_specs=(hbm, hbm),
        scratch_shapes=[
            pltpu.VMEM((width, rows), jnp.bfloat16),
            pltpu.VMEM(slot_map.shape, jnp.int32),
            pltpu.VMEM(row_weight.shape, jnp.float32),
            pltpu.SMEM(valid_rows.shape, jnp.int32),
            dma((4,)),
            pltpu.VMEM(panel, jnp.bfloat16),
            pltpu.VMEM(panel, jnp.bfloat16),
            pltpu.VMEM(panel, jnp.bfloat16),
            pltpu.VMEM((1, kept), jnp.float32),
            pltpu.VMEM((4, width, full), jnp.float32),
            dma((1,)), grid4, grid4, grid4, grid4, grid4, grid4, grid4, dma((2,)), dma((2,)), dma((2,)),
        ],
        compiler_params=pltpu.CompilerParams(
            collective_id=0, has_side_effects=True, vmem_limit_bytes=63 * 2**20
        ),
        cost_estimate=pl.CostEstimate(
            flops=2 * full * full * kept, bytes_accessed=8 * 2**20, transcendentals=0
        ),
    )(snapshots.T, slot_map, row_weight, valid_rows)
    return (mine + other).reshape(2 * width, full)


def solution(mesh):
    shape = dict(mesh.shape)
    use_kernel = shape == {"bi": 4, "bj": 4, "sl": 2}
    return jax.shard_map(
        fused if use_kernel else body,
        mesh=mesh,
        in_specs=(P("sl", ("bj", "bi")), P(("bj", "bi"), None), P("sl"), P("sl", None)),
        out_specs=P(("bi", "sl"), "bj"),
        check_vma=False,
    )
```

```python
import jax
import jax.numpy as jnp
from jax import lax
from jax.experimental import pallas as pl
from jax.experimental.pallas import tpu as pltpu
from jax.sharding import PartitionSpec as P

MESH = pl.DeviceIdType.MESH
CHUNKS = 3
LENT = 3


def nt(a, b):
    return lax.dot_general(a, b, (((1,), (1,)), ((), ())), preferred_element_type=jnp.float32)


def contract_rows(left_panel, right_panel):
    return lax.dot_general(
        left_panel, right_panel, (((0,), (0,)), ((), ())), preferred_element_type=jnp.float32
    )


def body(snapshots, slot_map, row_weight, valid_rows):
    local_rows = snapshots.shape[0]
    sources_here = valid_rows.shape[1]
    source_rows = local_rows // sources_here
    ordered = jnp.zeros_like(snapshots).at[:, slot_map[0]].set(snapshots)
    positions = jnp.arange(local_rows, dtype=jnp.int32)
    source = positions // source_rows
    within = positions % source_rows
    source_ids = jnp.arange(sources_here, dtype=jnp.int32)
    matches = source[:, None] == source_ids[None, :]
    row_limit = jnp.sum(jnp.where(matches, valid_rows[0][None, :], 0), axis=1)
    row_factor = jnp.where(within < row_limit, row_weight, jnp.zeros_like(row_weight))
    count_bi = lax.axis_size("bi")
    count_bj = lax.axis_size("bj")
    per_row = count_bj // count_bi
    row_count = ordered.shape[0]
    shard_width = ordered.shape[1]
    column_panel = lax.all_gather(ordered, "bi", axis=1, tiled=True)
    weighted_shard = (ordered.astype(jnp.float32) * row_factor[:, None]).astype(jnp.bfloat16)
    sectioned = weighted_shard.reshape(row_count, 1, 1, shard_width)
    moved = lax.all_to_all(
        lax.all_to_all(sectioned, "bj", split_axis=0, concat_axis=1, tiled=True),
        "bi",
        split_axis=1,
        concat_axis=2,
        tiled=True,
    )
    gathered = lax.all_gather(moved, "bj", axis=0, tiled=True)
    weighted = gathered.reshape(row_count, per_row * count_bi * shard_width)
    return lax.psum_scatter(
        contract_rows(weighted, column_panel), "sl", scatter_dimension=0, tiled=True
    )


def gram_kernel(
    snap_in, slot_in, weight_in, valid_in, mine, other,
    snap, slot, weight, valid, insem, colp, rowp, offl, wrow, acc,
    own_z, gsend, grecv, upsend, dnsend, rrecv, orecv, psend, ssend, srecv, ksem,
):
    r = lax.axis_index("bi")
    z = lax.axis_index("bj")
    s = lax.axis_index("sl")
    width, rows = snap.shape
    sources = valid.shape[1]
    src_rows = rows // sources
    kept = (sources - 1) * src_rows
    C = CHUNKS
    part = width // C
    diag = r == z
    not_diag = r != z
    low = z > 0
    high = z < 3

    loads = [
        pltpu.make_async_copy(src, dst, insem.at[i])
        for i, (src, dst) in enumerate(
            ((snap_in, snap), (slot_in, slot), (valid_in, valid), (weight_in, weight)))
    ]
    for load in loads:
        load.start()
    barrier = pltpu.get_barrier_semaphore()
    for k in (1, 2, 3):
        mate = (r + k) % 4
        pl.semaphore_signal(barrier, inc=1, device_id={"bi": mate}, device_id_type=MESH)
    pl.semaphore_signal(barrier, inc=1, device_id={"sl": 1 - s}, device_id_type=MESH)

    @pl.when(low)
    def _():
        pl.semaphore_signal(barrier, inc=1, device_id={"bj": z - 1}, device_id_type=MESH)

    @pl.when(high)
    def _():
        pl.semaphore_signal(barrier, inc=1, device_id={"bj": z + 1}, device_id_type=MESH)

    for load in loads:
        load.wait()
    place = lax.broadcasted_iota(jnp.int32, (width, width), 0)
    turn = (place == slot[...]).astype(jnp.float32).astype(jnp.bfloat16)
    turned = jnp.dot(turn, snap[...], preferred_element_type=jnp.float32).astype(jnp.bfloat16)
    start = jnp.int32(0)
    targets = []
    lane = lax.broadcasted_iota(jnp.int32, (1, src_rows), 1)
    for q in range(sources):
        count = valid[0, q]
        targets.append(jnp.where(lane < count, lane + start, -1))
        start = start + count
    target = jnp.concatenate(targets, axis=1)
    choose = (lax.broadcasted_iota(jnp.int32, (kept, rows), 0) == target)
    choose = choose.astype(jnp.float32).astype(jnp.bfloat16)
    w = weight[...].reshape(1, rows)
    hi = w.astype(jnp.bfloat16).astype(jnp.float32)
    mid = (w - hi).astype(jnp.bfloat16).astype(jnp.float32)
    low_bits = w - hi - mid
    pieces = jnp.concatenate([hi, mid, low_bits, jnp.zeros((13, rows), jnp.float32)], axis=0)
    packed = nt(jnp.concatenate([turned, pieces.astype(jnp.bfloat16)], axis=0), choose)
    colp[pl.ds(r, 1)] = packed[:width].astype(jnp.bfloat16).reshape(1, C, part, kept)
    wrow[...] = packed[width:width + 1] + packed[width + 1:width + 2] + packed[width + 2:width + 3]

    pl.semaphore_wait(barrier, 4 + (z + 3) // 4 + (6 - z) // 4)

    def to_plane(k, c):
        return pltpu.make_async_remote_copy(
            src_ref=colp.at[r, c], dst_ref=colp.at[r, c],
            send_sem=gsend.at[k, c], recv_sem=grecv.at[r, c],
            device_id={"bi": flip(k)}, device_id_type=MESH)

    def flip(k):
        x, y = r % 2, r // 2
        x = 1 - x if k % 2 else x
        y = 1 - y if k // 2 else y
        return 2 * y + x

    def along(src, dst, step, sends, recvs, b, c):
        return pltpu.make_async_remote_copy(
            src_ref=src.at[b, c], dst_ref=dst.at[b, c],
            send_sem=sends.at[b, c], recv_sem=recvs.at[b, c],
            device_id={"bj": z + step}, device_id_type=MESH)

    def up_row(src, b, c):
        return along(src, rowp, 1, upsend, rrecv, b, c)

    def dn_row(src, b, c):
        return along(src, rowp, -1, dnsend, rrecv, b, c)

    def own_off(step, sends, c):
        return pltpu.make_async_remote_copy(
            src_ref=colp.at[r, c], dst_ref=offl.at[z, c],
            send_sem=sends.at[z, c], recv_sem=orecv.at[z, c],
            device_id={"bj": z + step}, device_id_type=MESH)

    def hand(p, c):
        return pltpu.make_async_remote_copy(
            src_ref=offl.at[p, c], dst_ref=rowp.at[r, c],
            send_sem=psend.at[p, c], recv_sem=rrecv.at[r, c],
            device_id={"bi": p}, device_id_type=MESH)

    def got(buf, recvs, b, c):
        pltpu.make_async_remote_copy(
            src_ref=buf.at[b, c], dst_ref=buf.at[b, c],
            send_sem=own_z.at[0], recv_sem=recvs.at[b, c],
            device_id={"sl": 1 - s}, device_id_type=MESH).wait_recv()

    def act(condition, copy, drain):
        @pl.when(condition)
        def _():
            if drain:
                copy().wait_send()
            else:
                copy().start()

    down = (r - z + 3 + r // 3) // 4
    second = down * (3 - r // 3) + (1 - down) * (1 - (r + 2) // 3)
    third = down * 6 + (1 - down) * 3 - r - second
    lent = (1 - down) * 3
    natural = (r, second, third, lent)
    off_down = (r == 0)
    off_up = (r == 3)

    def send_own(c, drain):
        act(diag & low, lambda: dn_row(colp, r, c), drain)
        act(diag & high, lambda: up_row(colp, r, c), drain)
        act(off_down & low & (c < LENT), lambda: own_off(-1, dnsend, c), drain)
        act(off_up & high & (c < LENT), lambda: own_off(1, upsend, c), drain)
        for k in (1, 2):
            act(r >= 0, lambda: to_plane(k, c), drain)

    def relay(k, c):
        b = flip(k)
        return pltpu.make_async_remote_copy(
            src_ref=colp.at[b, c], dst_ref=colp.at[b, c],
            send_sem=gsend.at[3, c], recv_sem=grecv.at[b, c],
            device_id={"bi": flip(3 - k)}, device_id_type=MESH)

    def plane_step(k, c, drain):
        b = flip(k)
        if not drain:
            got(colp, grecv, b, c)
        if k != 3:
            act(c % 2 == k - 1, lambda: relay(k, c), drain)
        act(diag & low & ((b >= 1) | (c >= LENT)), lambda: dn_row(colp, b, c), drain)
        act(diag & high & ((b <= 2) | (c >= LENT)), lambda: up_row(colp, b, c), drain)

    def line_step(u, c, drain):
        p_dn = z + 1 + u

        @pl.when(off_down & (p_dn <= 3) & (c < LENT))
        def _():
            if not drain:
                got(offl, orecv, p_dn, c)
            act(low, lambda: along(offl, offl, -1, dnsend, orecv, p_dn, c), drain)
            act(r >= 0, lambda: hand(p_dn, c), drain)

        p_up = z - 1 - u

        @pl.when(off_up & (p_up >= 0) & (c < LENT))
        def _():
            if not drain:
                got(offl, orecv, p_up, c)
            act(high, lambda: along(offl, offl, 1, upsend, orecv, p_up, c), drain)
            act(r >= 0, lambda: hand(p_up, c), drain)

        natural_step(u, c, drain)

    def natural_step(u, c, drain):
        b = natural[u]

        @pl.when(not_diag)
        def _():
            if not drain:
                got(rowp, rrecv, b, c)
        act((z < r) & low, lambda: dn_row(rowp, b, c), drain)
        act((z > r) & high, lambda: up_row(rowp, b, c), drain)

    def over(step):
        def one(c, carry):
            step(c)
            return carry
        lax.fori_loop(0, C, one, 0)

    def to_sister(b):
        return pltpu.make_async_remote_copy(
            src_ref=acc.at[b], dst_ref=other.at[b % 2],
            send_sem=ssend.at[b % 2], recv_sem=srecv.at[b % 2],
            device_id={"sl": 1 - s}, device_id_type=MESH)

    def keep(b):
        return pltpu.make_async_copy(acc.at[b], mine.at[b % 2], ksem.at[b % 2])

    def multiply(b):
        @pl.when(diag)
        def _():
            rowp[pl.ds(b, 1)] = colp[pl.ds(b, 1)]
        block = rowp[pl.ds(b, 1)].reshape(width, kept).astype(jnp.float32)
        weighted = (block * wrow[...]).astype(jnp.bfloat16)
        acc[pl.ds(b, 1)] = nt(weighted, colp[...].reshape(4 * width, kept))[None]

        @pl.when(b // 2 != s)
        def _():
            to_sister(b).start()

        @pl.when(b // 2 == s)
        def _():
            keep(b).start()

    over(lambda c: send_own(c, False))

    def first(c):
        plane_step(1, c, False)
        plane_step(2, c, False)
        line_step(0, c, False)
    over(first)

    @pl.when(diag)
    def _():
        over(lambda c: plane_step(3, c, False))
    in_turn = (r == 0) | (r == 3)
    is_end = ((z == 0) & (r >= 1)) | ((z == 3) & (r <= 2))
    is_middle = jnp.logical_not(is_end)

    def far_block():
        @pl.when(not_diag)
        def _():
            over(lambda c: plane_step(3, c, False))

    def products(lo, hi):
        def one(i, carry):
            b = r + (i % 2) * (second - r) + (i // 2) * (third - r)
            multiply(b)
            return carry
        lax.fori_loop(lo, hi, one, 0)

    @pl.when(is_end & in_turn)
    def _():
        far_block()
        products(0, 1)

    @pl.when(in_turn)
    def _():
        def both(c):
            line_step(1, c, False)
            line_step(2, c, False)
        over(both)

    @pl.when(is_end & in_turn)
    def _():
        products(1, 3)

    @pl.when(jnp.logical_not(in_turn))
    def _():
        over(lambda c: line_step(1, c, False))

        @pl.when(is_end)
        def _():
            far_block()
            products(0, 2)
        over(lambda c: line_step(2, c, False))

        @pl.when(is_end)
        def _():
            products(2, 3)

    @pl.when(is_middle)
    def _():
        far_block()
        products(0, 3)

    def last(c):
        @pl.when(c >= LENT)
        def _():
            natural_step(3, c, False)

        @pl.when(not_diag & (c < LENT))
        def _():
            got(rowp, rrecv, lent, c)

    over(last)
    multiply(lent)

    for j in range(2):
        pltpu.make_async_remote_copy(
            src_ref=acc.at[j], dst_ref=other.at[j], send_sem=ssend.at[j], recv_sem=srecv.at[j],
            device_id={"sl": 1 - s}, device_id_type=MESH).wait()
        keep(2 * s + j).wait()

    def drain(c):
        send_own(c, True)
        for k in (1, 2, 3):
            plane_step(k, c, True)
        for u in range(3):
            line_step(u, c, True)

        @pl.when(c >= LENT)
        def _():
            natural_step(3, c, True)
    over(drain)


def fused(snapshots, slot_map, row_weight, valid_rows):
    rows, width = snapshots.shape
    sources = valid_rows.shape[1]
    hbm = pl.BlockSpec(memory_space=pltpu.HBM)
    kept = (sources - 1) * (rows // sources)
    panel = (4, CHUNKS, width // CHUNKS, kept)
    full = 4 * width
    dma = pltpu.SemaphoreType.DMA
    grid4 = dma((4, CHUNKS))
    half = jax.ShapeDtypeStruct((2, width, full), jnp.float32)
    mine, other = pl.pallas_call(
        gram_kernel,
        out_shape=(half, half),
        in_specs=[hbm] * 4,
        out_specs=(hbm, hbm),
        scratch_shapes=[
            pltpu.VMEM((width, rows), jnp.bfloat16),
            pltpu.VMEM(slot_map.shape, jnp.int32),
            pltpu.VMEM(row_weight.shape, jnp.float32),
            pltpu.SMEM(valid_rows.shape, jnp.int32),
            dma((4,)),
            pltpu.VMEM(panel, jnp.bfloat16),
            pltpu.VMEM(panel, jnp.bfloat16),
            pltpu.VMEM(panel, jnp.bfloat16),
            pltpu.VMEM((1, kept), jnp.float32),
            pltpu.VMEM((4, width, full), jnp.float32),
            dma((1,)), grid4, grid4, grid4, grid4, grid4, grid4, grid4, dma((2,)), dma((2,)), dma((2,)),
        ],
        compiler_params=pltpu.CompilerParams(
            collective_id=0, has_side_effects=True, vmem_limit_bytes=48 * 2**20
        ),
        cost_estimate=pl.CostEstimate(
            flops=2 * full * full * kept, bytes_accessed=8 * 2**20, transcendentals=0
        ),
    )(*(pltpu.with_memory_space_constraint(x, pltpu.HBM) for x in (snapshots.T, slot_map, row_weight, valid_rows)))
    return (mine + other).reshape(2 * width, full)


def solution(mesh):
    shape = dict(mesh.shape)
    use_kernel = shape == {"bi": 4, "bj": 4, "sl": 2}
    return jax.shard_map(
        fused if use_kernel else body,
        mesh=mesh,
        in_specs=(P("sl", ("bj", "bi")), P(("bj", "bi"), None), P("sl"), P("sl", None)),
        out_specs=P(("bi", "sl"), "bj"),
        check_vma=False,
    )
```

```python
import jax
import jax.numpy as jnp
from jax import lax
from jax.experimental import pallas as pl
from jax.experimental.pallas import tpu as pltpu
from jax.sharding import PartitionSpec as P

MESH = pl.DeviceIdType.MESH
CHUNKS = 4
LENT = 4


def nt(a, b):
    return lax.dot_general(a, b, (((1,), (1,)), ((), ())), preferred_element_type=jnp.float32)


def contract_rows(left_panel, right_panel):
    return lax.dot_general(
        left_panel, right_panel, (((0,), (0,)), ((), ())), preferred_element_type=jnp.float32
    )


def body(snapshots, slot_map, row_weight, valid_rows):
    local_rows = snapshots.shape[0]
    sources_here = valid_rows.shape[1]
    source_rows = local_rows // sources_here
    ordered = jnp.zeros_like(snapshots).at[:, slot_map[0]].set(snapshots)
    positions = jnp.arange(local_rows, dtype=jnp.int32)
    source = positions // source_rows
    within = positions % source_rows
    source_ids = jnp.arange(sources_here, dtype=jnp.int32)
    matches = source[:, None] == source_ids[None, :]
    row_limit = jnp.sum(jnp.where(matches, valid_rows[0][None, :], 0), axis=1)
    row_factor = jnp.where(within < row_limit, row_weight, jnp.zeros_like(row_weight))
    count_bi = lax.axis_size("bi")
    count_bj = lax.axis_size("bj")
    per_row = count_bj // count_bi
    row_count = ordered.shape[0]
    shard_width = ordered.shape[1]
    column_panel = lax.all_gather(ordered, "bi", axis=1, tiled=True)
    weighted_shard = (ordered.astype(jnp.float32) * row_factor[:, None]).astype(jnp.bfloat16)
    sectioned = weighted_shard.reshape(row_count, 1, 1, shard_width)
    moved = lax.all_to_all(
        lax.all_to_all(sectioned, "bj", split_axis=0, concat_axis=1, tiled=True),
        "bi",
        split_axis=1,
        concat_axis=2,
        tiled=True,
    )
    gathered = lax.all_gather(moved, "bj", axis=0, tiled=True)
    weighted = gathered.reshape(row_count, per_row * count_bi * shard_width)
    return lax.psum_scatter(
        contract_rows(weighted, column_panel), "sl", scatter_dimension=0, tiled=True
    )


def gram_kernel(
    snap_in, slot_in, weight_in, valid_in, mine, other,
    snap, slot, weight, valid, insem, colp, rowp, offl, wrow, acc,
    own_z, gsend, grecv, upsend, dnsend, rrecv, orecv, psend, ssend, srecv, ksem,
):
    r = lax.axis_index("bi")
    z = lax.axis_index("bj")
    s = lax.axis_index("sl")
    width, rows = snap.shape
    sources = valid.shape[1]
    src_rows = rows // sources
    kept = (sources - 1) * src_rows
    C = CHUNKS
    part = width // C
    diag = r == z
    not_diag = r != z
    low = z > 0
    high = z < 3

    loads = [
        pltpu.make_async_copy(src, dst, insem.at[i])
        for i, (src, dst) in enumerate(
            ((snap_in, snap), (slot_in, slot), (valid_in, valid), (weight_in, weight)))
    ]
    for load in loads:
        load.start()
    barrier = pltpu.get_barrier_semaphore()
    for k in (1, 2, 3):
        mate = (r + k) % 4
        pl.semaphore_signal(barrier, inc=1, device_id={"bi": mate}, device_id_type=MESH)
    pl.semaphore_signal(barrier, inc=1, device_id={"sl": 1 - s}, device_id_type=MESH)

    @pl.when(low)
    def _():
        pl.semaphore_signal(barrier, inc=1, device_id={"bj": z - 1}, device_id_type=MESH)

    @pl.when(high)
    def _():
        pl.semaphore_signal(barrier, inc=1, device_id={"bj": z + 1}, device_id_type=MESH)

    for load in loads:
        load.wait()
    place = lax.broadcasted_iota(jnp.int32, (width, width), 0)
    turn = (place == slot[...]).astype(jnp.float32).astype(jnp.bfloat16)
    turned = jnp.dot(turn, snap[...], preferred_element_type=jnp.float32).astype(jnp.bfloat16)
    start = jnp.int32(0)
    targets = []
    lane = lax.broadcasted_iota(jnp.int32, (1, src_rows), 1)
    for q in range(sources):
        count = valid[0, q]
        targets.append(jnp.where(lane < count, lane + start, -1))
        start = start + count
    target = jnp.concatenate(targets, axis=1)
    choose = (lax.broadcasted_iota(jnp.int32, (kept, rows), 0) == target)
    choose = choose.astype(jnp.float32).astype(jnp.bfloat16)
    w = weight[...].reshape(1, rows)
    hi = w.astype(jnp.bfloat16).astype(jnp.float32)
    mid = (w - hi).astype(jnp.bfloat16).astype(jnp.float32)
    low_bits = w - hi - mid
    pieces = jnp.concatenate([hi, mid, low_bits, jnp.zeros((13, rows), jnp.float32)], axis=0)
    packed = nt(jnp.concatenate([turned, pieces.astype(jnp.bfloat16)], axis=0), choose)
    colp[pl.ds(r, 1)] = packed[:width].astype(jnp.bfloat16).reshape(1, C, part, kept)
    wrow[...] = packed[width:width + 1] + packed[width + 1:width + 2] + packed[width + 2:width + 3]

    pl.semaphore_wait(barrier, 4 + (z + 3) // 4 + (6 - z) // 4)

    def to_plane(k, c):
        return pltpu.make_async_remote_copy(
            src_ref=colp.at[r, c], dst_ref=colp.at[r, c],
            send_sem=gsend.at[k, c], recv_sem=grecv.at[r, c],
            device_id={"bi": flip(k)}, device_id_type=MESH)

    def flip(k):
        x, y = r % 2, r // 2
        x = 1 - x if k % 2 else x
        y = 1 - y if k // 2 else y
        return 2 * y + x

    def along(src, dst, step, sends, recvs, b, c):
        return pltpu.make_async_remote_copy(
            src_ref=src.at[b, c], dst_ref=dst.at[b, c],
            send_sem=sends.at[b, c], recv_sem=recvs.at[b, c],
            device_id={"bj": z + step}, device_id_type=MESH)

    def up_row(src, b, c):
        return along(src, rowp, 1, upsend, rrecv, b, c)

    def dn_row(src, b, c):
        return along(src, rowp, -1, dnsend, rrecv, b, c)

    def own_off(step, sends, c):
        return pltpu.make_async_remote_copy(
            src_ref=colp.at[r, c], dst_ref=offl.at[z, c],
            send_sem=sends.at[z, c], recv_sem=orecv.at[z, c],
            device_id={"bj": z + step}, device_id_type=MESH)

    def hand(p, c):
        return pltpu.make_async_remote_copy(
            src_ref=offl.at[p, c], dst_ref=rowp.at[r, c],
            send_sem=psend.at[p, c], recv_sem=rrecv.at[r, c],
            device_id={"bi": p}, device_id_type=MESH)

    def got(buf, recvs, b, c):
        pltpu.make_async_remote_copy(
            src_ref=buf.at[b, c], dst_ref=buf.at[b, c],
            send_sem=own_z.at[0], recv_sem=recvs.at[b, c],
            device_id={"sl": 1 - s}, device_id_type=MESH).wait_recv()

    def act(condition, copy, drain):
        @pl.when(condition)
        def _():
            if drain:
                copy().wait_send()
            else:
                copy().start()

    down = (r - z + 3 + r // 3) // 4
    second = down * (3 - r // 3) + (1 - down) * (1 - (r + 2) // 3)
    third = down * 6 + (1 - down) * 3 - r - second
    lent = (1 - down) * 3
    natural = (r, second, third, lent)
    off_down = (r == 0)
    off_up = (r == 3)

    def send_own(c, drain):
        act(diag & low, lambda: dn_row(colp, r, c), drain)
        act(diag & high, lambda: up_row(colp, r, c), drain)
        act(off_down & low & (c < LENT), lambda: own_off(-1, dnsend, c), drain)
        act(off_up & high & (c < LENT), lambda: own_off(1, upsend, c), drain)
        for k in (1, 2):
            act(r >= 0, lambda: to_plane(k, c), drain)

    def relay(k, c):
        b = flip(k)
        return pltpu.make_async_remote_copy(
            src_ref=colp.at[b, c], dst_ref=colp.at[b, c],
            send_sem=gsend.at[3, c], recv_sem=grecv.at[b, c],
            device_id={"bi": flip(3 - k)}, device_id_type=MESH)

    def plane_step(k, c, drain):
        b = flip(k)
        if not drain:
            got(colp, grecv, b, c)
        if k != 3:
            act(c % 2 == k - 1, lambda: relay(k, c), drain)
        act(diag & low & ((b >= 1) | (c >= LENT)), lambda: dn_row(colp, b, c), drain)
        act(diag & high & ((b <= 2) | (c >= LENT)), lambda: up_row(colp, b, c), drain)

    def line_step(u, c, drain):
        p_dn = z + 1 + u

        @pl.when(off_down & (p_dn <= 3) & (c < LENT))
        def _():
            if not drain:
                got(offl, orecv, p_dn, c)
            act(low, lambda: along(offl, offl, -1, dnsend, orecv, p_dn, c), drain)
            act(r >= 0, lambda: hand(p_dn, c), drain)

        p_up = z - 1 - u

        @pl.when(off_up & (p_up >= 0) & (c < LENT))
        def _():
            if not drain:
                got(offl, orecv, p_up, c)
            act(high, lambda: along(offl, offl, 1, upsend, orecv, p_up, c), drain)
            act(r >= 0, lambda: hand(p_up, c), drain)

        natural_step(u, c, drain)

    def natural_step(u, c, drain):
        b = natural[u]

        @pl.when(not_diag)
        def _():
            if not drain:
                got(rowp, rrecv, b, c)
        act((z < r) & low, lambda: dn_row(rowp, b, c), drain)
        act((z > r) & high, lambda: up_row(rowp, b, c), drain)

    def over(step):
        def one(c, carry):
            step(c)
            return carry
        lax.fori_loop(0, C, one, 0)

    def to_sister(b):
        return pltpu.make_async_remote_copy(
            src_ref=acc.at[b], dst_ref=other.at[b % 2],
            send_sem=ssend.at[b % 2], recv_sem=srecv.at[b % 2],
            device_id={"sl": 1 - s}, device_id_type=MESH)

    def keep(b):
        return pltpu.make_async_copy(acc.at[b], mine.at[b % 2], ksem.at[b % 2])

    def multiply(b):
        @pl.when(diag)
        def _():
            rowp[pl.ds(b, 1)] = colp[pl.ds(b, 1)]
        block = rowp[pl.ds(b, 1)].reshape(width, kept).astype(jnp.float32)
        weighted = (block * wrow[...]).astype(jnp.bfloat16)
        acc[pl.ds(b, 1)] = nt(weighted, colp[...].reshape(4 * width, kept))[None]

        @pl.when(b // 2 != s)
        def _():
            to_sister(b).start()

        @pl.when(b // 2 == s)
        def _():
            keep(b).start()

    over(lambda c: send_own(c, False))

    def first(c):
        plane_step(1, c, False)
        plane_step(2, c, False)
        line_step(0, c, False)
    over(first)

    @pl.when(diag)
    def _():
        over(lambda c: plane_step(3, c, False))
    in_turn = (r == 0) | (r == 3)
    is_end = ((z == 0) & (r >= 1)) | ((z == 3) & (r <= 2))
    is_middle = jnp.logical_not(is_end)

    def far_block():
        @pl.when(not_diag)
        def _():
            over(lambda c: plane_step(3, c, False))

    def products(lo, hi):
        def one(i, carry):
            b = r + (i % 2) * (second - r) + (i // 2) * (third - r)
            multiply(b)
            return carry
        lax.fori_loop(lo, hi, one, 0)

    @pl.when(is_end & in_turn)
    def _():
        far_block()
        products(0, 1)

    @pl.when(in_turn)
    def _():
        def both(c):
            line_step(1, c, False)
            line_step(2, c, False)
        over(both)

    @pl.when(is_end & in_turn)
    def _():
        products(1, 3)

    @pl.when(jnp.logical_not(in_turn))
    def _():
        over(lambda c: line_step(1, c, False))

        @pl.when(is_end)
        def _():
            far_block()
            products(0, 2)
        over(lambda c: line_step(2, c, False))

        @pl.when(is_end)
        def _():
            products(2, 3)

    @pl.when(is_middle)
    def _():
        far_block()
        products(0, 3)

    def last(c):
        @pl.when(c >= LENT)
        def _():
            natural_step(3, c, False)

        @pl.when(not_diag & (c < LENT))
        def _():
            got(rowp, rrecv, lent, c)

    over(last)
    multiply(lent)

    for j in range(2):
        pltpu.make_async_remote_copy(
            src_ref=acc.at[j], dst_ref=other.at[j], send_sem=ssend.at[j], recv_sem=srecv.at[j],
            device_id={"sl": 1 - s}, device_id_type=MESH).wait()
        keep(2 * s + j).wait()

    def drain(c):
        send_own(c, True)
        for k in (1, 2, 3):
            plane_step(k, c, True)
        for u in range(3):
            line_step(u, c, True)

        @pl.when(c >= LENT)
        def _():
            natural_step(3, c, True)
    over(drain)


def fused(snapshots, slot_map, row_weight, valid_rows):
    rows, width = snapshots.shape
    sources = valid_rows.shape[1]
    hbm = pl.BlockSpec(memory_space=pltpu.HBM)
    kept = (sources - 1) * (rows // sources)
    panel = (4, CHUNKS, width // CHUNKS, kept)
    full = 4 * width
    dma = pltpu.SemaphoreType.DMA
    grid4 = dma((4, CHUNKS))
    half = jax.ShapeDtypeStruct((2, width, full), jnp.float32)
    mine, other = pl.pallas_call(
        gram_kernel,
        out_shape=(half, half),
        in_specs=[hbm] * 4,
        out_specs=(hbm, hbm),
        scratch_shapes=[
            pltpu.VMEM((width, rows), jnp.bfloat16),
            pltpu.VMEM(slot_map.shape, jnp.int32),
            pltpu.VMEM(row_weight.shape, jnp.float32),
            pltpu.SMEM(valid_rows.shape, jnp.int32),
            dma((4,)),
            pltpu.VMEM(panel, jnp.bfloat16),
            pltpu.VMEM(panel, jnp.bfloat16),
            pltpu.VMEM(panel, jnp.bfloat16),
            pltpu.VMEM((1, kept), jnp.float32),
            pltpu.VMEM((4, width, full), jnp.float32),
            dma((1,)), grid4, grid4, grid4, grid4, grid4, grid4, grid4, dma((2,)), dma((2,)), dma((2,)),
        ],
        compiler_params=pltpu.CompilerParams(
            collective_id=0, has_side_effects=True, vmem_limit_bytes=48 * 2**20
        ),
        cost_estimate=pl.CostEstimate(
            flops=2 * full * full * kept, bytes_accessed=8 * 2**20, transcendentals=0
        ),
    )(*(pltpu.with_memory_space_constraint(x, pltpu.HBM) for x in (snapshots.T, slot_map, row_weight, valid_rows)))
    return (mine + other).reshape(2 * width, full)


def solution(mesh):
    shape = dict(mesh.shape)
    use_kernel = shape == {"bi": 4, "bj": 4, "sl": 2}
    return jax.shard_map(
        fused if use_kernel else body,
        mesh=mesh,
        in_specs=(P("sl", ("bj", "bi")), P(("bj", "bi"), None), P("sl"), P("sl", None)),
        out_specs=P(("bi", "sl"), "bj"),
        check_vma=False,
    )
```
